32 devices in a mesh: ang: 16 (over z, x, core), pix: 2 (over y).
Axes of the slice: x: 2, y: 2, z: 4, core: 2. Of those that a mesh axis runs over, the one named last changes fastest.
Arguments:
- grads: bfloat16 [2, 4096, 32, 512], P(None, 'ang', 'pix')
- circle_pos: int32 [4096], replicated, may hold values from 0 to 4095, as said below
- harmonics: int32 [256], replicated, may hold values from 0 to 4095, as said below
- support: int32 [32, 512], replicated, may hold values 0 or 1
Outputs:
- update: bfloat16 [2, 4096, 32, 512], P(None, 'ang', 'pix')
- harmonic_rms: float32 [256], replicated
The draws below stay inside these ranges and needn't reach their ends.
Inputs may be any that keep to these rules, and one draw needn't show every extreme that they name: `circle_pos`: the stored angles form 64 aligned blocks of 64 rows; block b holds the circle positions r_b + 64 * j for j = 0 to 63 in this order, and the 64 values r_b are distinct. `harmonics`: 256 distinct harmonic numbers, among them 0 and 4095.
All inputs are finite; a program needn't handle non-finite values.
Results may differ from the reference program's by a relative error of at most 0.015.
Values may be sent and summed in bfloat16 or wider, within the bound.
A program may use at most 192 MiB of HBM per device.

```python
import math
import jax
import jax.numpy as jnp
from jax import lax

A1 = 64
A2 = 64
K = 256
W = 512
ROWS = 32


def circle_list(key):
    residues = jax.random.permutation(jax.random.fold_in(key, 7), A1).astype(jnp.int32)
    offsets = jnp.arange(A2, dtype=jnp.int32) * A1
    return (residues[:, None] + offsets[None, :]).reshape(-1)


def harmonic_order(key):
    return jax.random.permutation(jax.random.fold_in(key, 11), A1 * A2 - 2).astype(jnp.int32) + 1


def draw_circle_pos(key, part):
    return circle_list(key)


def draw_harmonics(key, part):
    inner = harmonic_order(key)[:K - 2]
    chosen = jnp.concatenate([jnp.array([0, A1 * A2 - 1], jnp.int32), inner])
    return jax.random.permutation(jax.random.fold_in(key, 23), chosen)


def draw_grads(key, part):
    subkeys = jax.random.split(jax.random.fold_in(key, 31), 5)
    cycle_total = A1 * A2
    row_ramp = 3.0 ** (jnp.arange(ROWS, dtype=jnp.float32) / (ROWS - 1))
    row_factor = jnp.exp(jax.random.uniform(subkeys[0], (ROWS,), jnp.float32, 0.0, math.log(3.3)))
    col_factor = jnp.exp(jax.random.uniform(subkeys[1], (W,), jnp.float32, 0.0, math.log(3.3)))
    pixel_scale = (row_ramp * row_factor)[:, None] * col_factor[None, :]
    full_shape = (2, cycle_total, ROWS, W)
    positions = circle_list(key)
    order = harmonic_order(key)
    chosen_harmonics = jnp.concatenate([order[K - 2:K], order[:4]])
    amplitudes = [0.8, 0.8, 0.04, 0.06, 0.08, 0.1]
    offsets = jax.random.uniform(subkeys[4], (6, ROWS, W), jnp.float32, -math.pi, math.pi)
    coherent_re = jnp.zeros((cycle_total, ROWS, W), jnp.float32)
    coherent_im = jnp.zeros((cycle_total, ROWS, W), jnp.float32)
    for term_index in range(6):
        turn_count = chosen_harmonics[term_index] * positions % cycle_total
        phase_angle = turn_count.astype(jnp.float32) * (2.0 * math.pi / cycle_total)
        circle_cos = jnp.cos(phase_angle)[:, None, None]
        circle_sin = jnp.sin(phase_angle)[:, None, None]
        pixel_cos = jnp.cos(offsets[term_index])[None]
        pixel_sin = jnp.sin(offsets[term_index])[None]
        coherent_re = coherent_re + amplitudes[term_index] * (circle_cos * pixel_cos - circle_sin * pixel_sin)
        coherent_im = coherent_im + amplitudes[term_index] * (circle_sin * pixel_cos + circle_cos * pixel_sin)
    coherent = jnp.stack((coherent_re, coherent_im))
    values = pixel_scale[None, None] * (jax.random.normal(subkeys[2], full_shape, jnp.float32) + coherent)
    return values.astype(jnp.bfloat16)


def touch_ends(result, stream_key, low, high):
    index_at = [jax.random.randint(jax.random.fold_in(stream_key, axis), (), 0, length) for axis, length in enumerate(result.shape)]
    widest = result.shape.index(max(result.shape))
    beside = index_at[:widest] + [(index_at[widest] + 1) % result.shape[widest]] + index_at[widest + 1:]
    return result.at[tuple(index_at)].set(low).at[tuple(beside)].set(high)


def setup_inputs(seed: int = 0) -> dict:
    streams_of = jax.random.split(jax.random.key(seed), 5)
    return {
        "grads": draw_grads(jax.random.fold_in(streams_of[4], 71), 0),
        "circle_pos": draw_circle_pos(jax.random.fold_in(streams_of[4], 71), 0),
        "harmonics": draw_harmonics(jax.random.fold_in(streams_of[4], 71), 0),
        "support": touch_ends((jax.random.randint(streams_of[3], (ROWS, W), 0, 4) < 3).astype(jnp.int32), jax.random.fold_in(streams_of[3], 1), 0, 1),
    }


def reference(grads, circle_pos, harmonics, support):
    angle_count = circle_pos.shape[0]
    kept_count = harmonics.shape[0]
    row_count = grads.shape[2]
    col_count = grads.shape[3]
    group_count = row_count // 8
    blocked = jnp.moveaxis(grads.reshape(2, angle_count, group_count, 8, col_count), 2, 0)

    def forward(portion):
        field = lax.complex(portion[0].astype(jnp.float32), portion[1].astype(jnp.float32))
        on_circle = jnp.zeros_like(field).at[circle_pos].set(field)
        spectrum = jnp.fft.fft(on_circle, axis=0)[harmonics] / jnp.sqrt(jnp.float32(angle_count))
        return jnp.stack((jnp.real(spectrum), jnp.imag(spectrum)))
    coefficients = lax.map(forward, blocked)
    weight = support.astype(jnp.float32).reshape(group_count, 1, 1, 8, col_count)
    square_sums = lax.optimization_barrier(jnp.sum(weight * coefficients * coefficients, axis=(0, 1, 3, 4)))
    harmonic_rms = jnp.sqrt(square_sums / (row_count * col_count) + 1e-06)
    step_field = weight * coefficients / harmonic_rms[None, None, :, None, None]

    def backward(portion):
        values = lax.complex(portion[0], portion[1])
        spectrum = jnp.zeros((angle_count,) + values.shape[1:], values.dtype).at[harmonics].set(values)
        on_circle = jnp.fft.ifft(spectrum, axis=0) * angle_count
        picked = on_circle[circle_pos] / jnp.sqrt(jnp.float32(kept_count))
        return jnp.stack((jnp.real(picked), jnp.imag(picked))).astype(jnp.bfloat16)
    update = lax.map(backward, step_field)
    update = jnp.moveaxis(update, 0, 2).reshape(2, angle_count, row_count, col_count)
    return (update, harmonic_rms)
```

```python
import math

import jax
import jax.numpy as jnp
from jax import lax
from jax.experimental import pallas as pl
from jax.experimental.pallas import tpu as pltpu
from jax.sharding import PartitionSpec as P


def phase_table(harmonics, positions, modulus):
    radians = ((harmonics[:, None] * positions[None, :]) % modulus).astype(jnp.float32) * (2.0 * math.pi / modulus)
    cos, sin = jnp.cos(radians), jnp.sin(radians)
    return jnp.concatenate((jnp.concatenate((cos, sin), 1), jnp.concatenate((-sin, cos), 1)), 0)


def split_parts(value):
    high = lax.reduce_precision(value, 8, 7)
    return (high.astype(jnp.bfloat16), (value - high).astype(jnp.bfloat16))


def table_einsum(form, table, right):
    return sum(
        jnp.einsum(form, piece, right, preferred_element_type=jnp.float32) for piece in split_parts(table)
    )


def body(grads, circle_pos, harmonics, support):
    ang_count = lax.axis_size("ang")
    angle_local, row_pix, col_count = grads.shape[1:]
    row_local = row_pix // ang_count
    angle_count = circle_pos.shape[0]
    kept_count = harmonics.shape[0]
    me = lax.axis_index("ang")
    row_start = lax.axis_index("pix") * row_pix + me * row_local
    weight = lax.dynamic_slice_in_dim(support, row_start, row_local, 0).astype(jnp.float32)
    cell_count = float(row_pix * lax.axis_size("pix") * col_count)
    positions = lax.dynamic_slice_in_dim(circle_pos, me * angle_local, angle_local, 0)
    table = phase_table(harmonics, positions, angle_count)
    flat = grads.reshape(2 * angle_local, row_pix, col_count)
    partial = table_einsum("ka,arc->rkc", table, flat)
    coef = lax.psum_scatter(partial, "ang", scatter_dimension=0, tiled=True)
    coef = coef * (weight[:, None, :] * (1.0 / math.sqrt(angle_count)))
    squares = jnp.sum(coef * coef, axis=(0, 2))
    totals = lax.psum(squares[:kept_count] + squares[kept_count:], ("ang", "pix"))
    harmonic_rms = jnp.sqrt(totals / cell_count + 1e-06)
    every = lax.all_gather(coef.astype(jnp.bfloat16), "ang", axis=0, tiled=True)
    scale = (1.0 / math.sqrt(kept_count)) / harmonic_rms
    back = table * jnp.concatenate((scale, scale))[:, None]
    update = table_einsum("ka,rkc->arc", back, every).astype(jnp.bfloat16)
    return (update.reshape(grads.shape), harmonic_rms)


MESH = pl.DeviceIdType.MESH
ORDER = ((1, 3, 0), (1, 0, 0), (0, 3, 1), (0, 0, 1), (1, 3, 1), (1, 0, 1),
         (1, 2, 0), (1, 1, 0), (0, 2, 1), (0, 1, 1), (1, 2, 1), (1, 1, 1))


def starts():
    up, down, result = 0, 0, {}
    for half, t, rel in ORDER:
        result[half, t, rel] = (up, down)
        up += t > 0
        down += t < 3
    return result


def item_of(half, t, rel):
    return t if half == 0 else 4 + 2 * t + rel


def reduce_gather(grads_ref, high_ref, low_ref, weight_ref, out_ref, total_ref,
                  core_out, core_in, held, x_out, x_in, z_out, z_in, b_out, b_in, gathered, squares, y_in,
                  core_send, core_recv, x_send, x_recv, z_send, z_recv, b_send, b_recv,
                  gather_send, gather_recv, out_sem, y_send, y_recv):
    me = lax.axis_index("ang")
    pix = lax.axis_index("pix")
    z, x, c = me // 4, (me // 2) % 2, me % 2
    sibling = (z * 4 + x * 2 + 1 - c, pix)
    beside = (z * 4 + (1 - x) * 2 + c, pix)
    across = (me, 1 - pix)

    barrier = pltpu.get_barrier_semaphore()
    for device in (sibling, beside, across):
        pl.semaphore_signal(barrier, inc=1, device_id=device, device_id_type=MESH)

    @pl.when(z < 3)
    def _():
        pl.semaphore_signal(barrier, inc=1, device_id=(me + 4, pix), device_id_type=MESH)

    @pl.when(z > 0)
    def _():
        pl.semaphore_signal(barrier, inc=1, device_id=(me - 4, pix), device_id_type=MESH)

    inner = (z > 0) & (z < 3)

    @pl.when(inner)
    def _():
        pl.semaphore_wait(barrier, 5)

    @pl.when(jnp.logical_not(inner))
    def _():
        pl.semaphore_wait(barrier, 4)

    def unit(half, t, rel, own):
        xx = x if rel else 1 - x
        cc = c if own else 1 - c
        return (t * 4 + xx * 2 + cc) * 2 + half

    def remote(src, dst, send, recv, device):
        return pltpu.make_async_remote_copy(
            src_ref=src, dst_ref=dst, send_sem=send, recv_sem=recv, device_id=device, device_id_type=MESH)

    def core_copy(j):
        return remote(core_out.at[j], core_in.at[j], core_send.at[j], core_recv.at[j], sibling)

    def x_copy(t):
        return remote(x_out.at[t], x_in.at[t], x_send.at[t], x_recv.at[t], beside)

    def lanes(half):
        return pl.ds(half * 256, 256)

    def out_copy(u, half):
        return pltpu.make_async_copy(gathered.at[u], out_ref.at[u // 2, :, lanes(half)], out_sem.at[u])

    def partial(u, half):
        value = grads_ref[u // 2, :, lanes(half)]
        return (jnp.dot(high_ref[...], value, preferred_element_type=jnp.float32)
                + jnp.dot(low_ref[...], value, preferred_element_type=jnp.float32))

    def nth(i):
        return (i % 2) * (i // 2) + (1 - i % 2) * (3 - i // 2)

    def send_core(half, rel):
        @pl.loop(0, 4)
        def _(i):
            t = nth(i)
            j = (t * 2 + rel) * 2 + half
            core_out[j] = partial(unit(half, t, rel, False), half).astype(jnp.bfloat16)
            core_copy(j).start()

    def keep(half, rel):
        @pl.loop(0, 4)
        def _(i):
            t = nth(i)
            j = (t * 2 + rel) * 2 + half
            value = partial(unit(half, t, rel, True), half)
            core_copy(j).wait_recv()
            value = value + core_in[j].astype(jnp.float32)
            if half == 0 and rel == 0:
                x_out[t] = value.astype(jnp.bfloat16)
                x_copy(t).start()
            else:
                held[item_of(half, t, rel)] = value

    send_core(0, 0)
    send_core(1, 0)
    keep(0, 0)
    keep(1, 0)
    send_core(0, 1)
    send_core(1, 1)
    keep(0, 1)
    keep(1, 1)

    squares[...] = jnp.zeros_like(squares)

    def at_hand(u, half):
        out_copy(u, half).start()

        @pl.loop(0, 8)
        def _(i):
            rows = pl.ds(pl.multiple_of(i * 32, 32), 32)
            lower = pl.ds(pl.multiple_of(i * 32 + 256, 32), 32)
            re = gathered[u, rows, :].astype(jnp.float32)
            im = gathered[u, lower, :].astype(jnp.float32)
            both = re * re + im * im
            squares[rows, :] += both[:, :128] + both[:, 128:]

    def add_up(target, at, sources, weight):
        @pl.loop(0, 16)
        def _(i):
            rows = pl.ds(pl.multiple_of(i * 32, 32), 32)
            value = None
            for ref, index in sources:
                term = ref[index + (rows, slice(None))].astype(jnp.float32)
                value = term if value is None else value + term
            if weight is not None:
                value = value * weight_ref[weight]
            target[at, rows, :] = value.astype(jnp.bfloat16)

    begin = starts()

    def run(zz):
        sent = []
        events = []

        def z_copy(k, way):
            return remote(z_out.at[k], z_in.at[way, k], z_send.at[k], z_recv.at[way, k],
                          (me + 4 if way == 0 else me - 4, pix))

        def b_copy():
            return remote(b_out.at[0], b_in.at[0], b_send.at[0], b_recv.at[0], beside)

        def gather_copy(u, way):
            device = (None, None, beside, sibling)[way] or (me + 4 if way == 0 else me - 4, pix)
            return remote(gathered.at[u], gathered.at[u], gather_send.at[way, u], gather_recv.at[u], device)

        def arrive(u):
            gather_copy(u, 3).wait_recv()

        def start(copy):
            copy.start()
            sent.append(copy)

        def onward(u, ways):
            for way in ways:
                start(gather_copy(u, way))

        def z_sources(half, t, rel):
            k = item_of(half, t, rel)
            sources = [(held, (k,))]
            if half == 0:
                x_copy(t).wait_recv()
                sources.append((x_in, (t,)))
            if zz > 0 and t >= zz:
                z_copy(k, 0).wait_recv()
                sources.append((z_in, (0, k)))
            if zz < 3 and t <= zz:
                z_copy(k, 1).wait_recv()
                sources.append((z_in, (1, k)))
            return sources

        def away(t):
            ways = []
            if zz < 3 and t <= zz:
                ways.append(0)
            if zz > 0 and t >= zz:
                ways.append(1)
            return ways

        def pass_on(half, t, rel):
            k = item_of(half, t, rel)
            add_up(z_out, k, z_sources(half, t, rel), None)
            start(z_copy(k, 0 if t > zz else 1))

        def cross():
            add_up(b_out, 0, z_sources(1, zz, 0), None)
            start(b_copy())

        def finish(half):
            sources = z_sources(half, zz, 1)
            if half == 1:
                b_copy().wait_recv()
                sources.append((b_in, (0,)))
            u = unit(half, zz, 1, True)
            add_up(gathered, u, sources, u)
            onward(u, [2] + away(zz) + [3])
            at_hand(u, half)

        def forward(half, t, rel, ways):
            u = unit(half, t, rel, True)
            arrive(u)
            onward(u, ways + [3])
            at_hand(u, half)

        def from_core(half, t, rel):
            u = unit(half, t, rel, False)
            arrive(u)
            at_hand(u, half)

        def put(step, rank, action, *args):
            events.append((step, rank, len(events), action, args))

        def got(step, half, t, rel):
            put(step + 2, 3, from_core, half, t, rel)

        ends = {}
        for half, t, rel in ORDER:
            up, down = begin[half, t, rel]
            ends[half, t, rel] = max(up + t if t > 0 else 0, down + 3 - t if t < 3 else 0)
            if t != zz:
                put(up + zz if t > zz else down + 3 - zz, 0, pass_on, half, t, rel)
        for t in range(4):
            far = abs(zz - t)
            step = ends[0, t, 1]
            if far == 0:
                put(step, 1, finish, 0)
            else:
                put(step + far, 1, forward, 0, t, 1, [2] + away(t))
            got(step + far, 0, t, 1)
            put(step + far + 1, 2, forward, 0, t, 0, [])
            got(step + far + 1, 0, t, 0)
            step = max(ends[1, t, 1], ends[1, t, 0] + 1)
            if far == 0:
                put(ends[1, t, 0], 0, cross)
                put(step, 1, finish, 1)
            else:
                put(step + far, 1, forward, 1, t, 1, away(t))
            got(step + far, 1, t, 1)
            put(step + far + 1, 1, forward, 1, t, 0, away(t))
            got(step + far + 1, 1, t, 0)
        for event in sorted(events, key=lambda entry: entry[:3]):
            event[3](*event[4])
        for copy in sent:
            copy.wait_send()

    for zz in range(4):
        pl.when(z == zz)(lambda zz=zz: run(zz))

    y_copy = remote(squares, y_in, y_send, y_recv, across)
    y_copy.start()

    @pl.loop(0, 16)
    def _(j):
        core_copy(j).wait_send()

    @pl.loop(0, 4)
    def _(t):
        x_copy(t).wait_send()

    @pl.loop(0, 16)
    def _(r):
        out_copy(2 * r, 0).wait()
        out_copy(2 * r + 1, 1).wait()

    y_copy.wait()
    total_ref[...] = squares[...] + y_in[...]


def gathered_coefficients(units, table, weight):
    high, low = split_parts(table)
    rows, cols = units.shape[1], units.shape[2] // 2
    block = lambda n: pltpu.VMEM((n, rows, cols), jnp.bfloat16)
    dma = pltpu.SemaphoreType.DMA
    vmem = pl.BlockSpec(memory_space=pltpu.VMEM)
    return pl.pallas_call(
        reduce_gather,
        out_shape=(jax.ShapeDtypeStruct(units.shape, jnp.bfloat16),
                   jax.ShapeDtypeStruct((rows // 2, 128), jnp.float32)),
        in_specs=[vmem] * 4,
        out_specs=(pl.BlockSpec(memory_space=pl.ANY), vmem),
        scratch_shapes=[
            block(16), block(16), pltpu.VMEM((12, rows, cols), jnp.float32), block(4), block(4),
            block(12), pltpu.VMEM((2, 12, rows, cols), jnp.bfloat16), block(1), block(1), block(32),
            pltpu.VMEM((rows // 2, 128), jnp.float32), pltpu.VMEM((rows // 2, 128), jnp.float32),
            dma((16,)), dma((16,)), dma((4,)), dma((4,)), dma((12,)), dma((2, 12)), dma((1,)), dma((1,)),
            dma((4, 32)), dma((32,)), dma((32,)), dma, dma,
        ],
        compiler_params=pltpu.CompilerParams(
            collective_id=0, has_side_effects=True, vmem_limit_bytes=58 * 2**20),
    )(units, high, low, weight)


def kernel_path(grads, circle_pos, harmonics, support):
    angle_local, row_pix, col_count = grads.shape[1:]
    angle_count = circle_pos.shape[0]
    kept_count = harmonics.shape[0]
    halves, lanes = 2, col_count // 2
    me = lax.axis_index("ang")
    positions = lax.dynamic_slice_in_dim(circle_pos, me * angle_local, angle_local, 0)
    table = phase_table(harmonics, positions, angle_count)
    units = grads.reshape(2 * angle_local, row_pix, col_count).transpose(1, 0, 2)
    weight = lax.dynamic_slice_in_dim(support, lax.axis_index("pix") * row_pix, row_pix, 0).astype(jnp.float32)
    weight = (weight * (1.0 / math.sqrt(angle_count))).reshape(row_pix * halves, 1, lanes)
    every, squares = gathered_coefficients(units, table, weight)
    cell_count = float(row_pix * lax.axis_size("pix") * col_count)
    harmonic_rms = jnp.sqrt(jnp.sum(squares, axis=1) / cell_count + 1e-06)
    scale = (1.0 / math.sqrt(kept_count)) / harmonic_rms
    back = table * jnp.concatenate((scale, scale))[:, None]
    update = jnp.einsum("ka,rkc->arc", back.astype(jnp.bfloat16), every, preferred_element_type=jnp.float32)
    return (update.astype(jnp.bfloat16).reshape(grads.shape), harmonic_rms)


def chosen(grads, circle_pos, harmonics, support):
    sizes = (lax.axis_size("ang"), lax.axis_size("pix"), harmonics.shape[0]) + grads.shape[1:]
    fits = sizes == (16, 2, 256, 256, 16, 512)
    return (kernel_path if fits else body)(grads, circle_pos, harmonics, support)


def solution(mesh):
    return jax.shard_map(
        chosen,
        mesh=mesh,
        in_specs=(P(None, "ang", "pix", None), P(), P(), P()),
        out_specs=(P(None, "ang", "pix", None), P()),
        check_vma=False,
    )
```

```python
import math

import jax
import jax.numpy as jnp
from jax import lax
from jax.experimental import pallas as pl
from jax.experimental.pallas import tpu as pltpu
from jax.sharding import PartitionSpec as P


def phase_table(harmonics, positions, modulus):
    radians = ((harmonics[:, None] * positions[None, :]) % modulus).astype(jnp.float32) * (2.0 * math.pi / modulus)
    cos, sin = jnp.cos(radians), jnp.sin(radians)
    return jnp.concatenate((jnp.concatenate((cos, sin), 1), jnp.concatenate((-sin, cos), 1)), 0)


def split_parts(value):
    high = lax.reduce_precision(value, 8, 7)
    return (high.astype(jnp.bfloat16), (value - high).astype(jnp.bfloat16))


def table_einsum(form, table, right):
    return sum(
        jnp.einsum(form, piece, right, preferred_element_type=jnp.float32) for piece in split_parts(table)
    )


def body(grads, circle_pos, harmonics, support):
    ang_count = lax.axis_size("ang")
    angle_local, row_pix, col_count = grads.shape[1:]
    row_local = row_pix // ang_count
    angle_count = circle_pos.shape[0]
    kept_count = harmonics.shape[0]
    me = lax.axis_index("ang")
    row_start = lax.axis_index("pix") * row_pix + me * row_local
    weight = lax.dynamic_slice_in_dim(support, row_start, row_local, 0).astype(jnp.float32)
    cell_count = float(row_pix * lax.axis_size("pix") * col_count)
    positions = lax.dynamic_slice_in_dim(circle_pos, me * angle_local, angle_local, 0)
    table = phase_table(harmonics, positions, angle_count)
    flat = grads.reshape(2 * angle_local, row_pix, col_count)
    partial = table_einsum("ka,arc->rkc", table, flat)
    coef = lax.psum_scatter(partial, "ang", scatter_dimension=0, tiled=True)
    coef = coef * (weight[:, None, :] * (1.0 / math.sqrt(angle_count)))
    squares = jnp.sum(coef * coef, axis=(0, 2))
    totals = lax.psum(squares[:kept_count] + squares[kept_count:], ("ang", "pix"))
    harmonic_rms = jnp.sqrt(totals / cell_count + 1e-06)
    every = lax.all_gather(coef.astype(jnp.bfloat16), "ang", axis=0, tiled=True)
    scale = (1.0 / math.sqrt(kept_count)) / harmonic_rms
    back = table * jnp.concatenate((scale, scale))[:, None]
    update = table_einsum("ka,rkc->arc", back, every).astype(jnp.bfloat16)
    return (update.reshape(grads.shape), harmonic_rms)


MESH = pl.DeviceIdType.MESH
ORDER = ((1, 3, 0), (1, 0, 0), (0, 3, 1), (0, 0, 1), (1, 3, 1), (1, 0, 1),
         (1, 2, 0), (1, 1, 0), (0, 2, 1), (0, 1, 1), (1, 2, 1), (1, 1, 1))


def starts():
    up, down, result = 0, 0, {}
    for half, t, rel in ORDER:
        result[half, t, rel] = (up, down)
        up += t > 0
        down += t < 3
    return result


def item_of(half, t, rel):
    return t if half == 0 else 4 + 2 * t + rel


def reduce_gather(grads_ref, high_ref, low_ref, weight_ref, out_ref, total_ref,
                  core_out, core_in, held, x_out, x_in, z_out, z_in, b_out, b_in, gathered, squares, y_in,
                  core_send, core_recv, x_send, x_recv, z_send, z_recv, b_send, b_recv,
                  gather_send, gather_recv, out_sem, y_send, y_recv):
    me = lax.axis_index("ang")
    pix = lax.axis_index("pix")
    z, x, c = me // 4, (me // 2) % 2, me % 2
    sibling = (z * 4 + x * 2 + 1 - c, pix)
    beside = (z * 4 + (1 - x) * 2 + c, pix)
    across = (me, 1 - pix)

    barrier = pltpu.get_barrier_semaphore()
    for device in (sibling, beside, across):
        pl.semaphore_signal(barrier, inc=1, device_id=device, device_id_type=MESH)

    @pl.when(z < 3)
    def _():
        pl.semaphore_signal(barrier, inc=1, device_id=(me + 4, pix), device_id_type=MESH)

    @pl.when(z > 0)
    def _():
        pl.semaphore_signal(barrier, inc=1, device_id=(me - 4, pix), device_id_type=MESH)

    inner = (z > 0) & (z < 3)

    @pl.when(inner)
    def _():
        pl.semaphore_wait(barrier, 5)

    @pl.when(jnp.logical_not(inner))
    def _():
        pl.semaphore_wait(barrier, 4)

    def unit(half, t, rel, own):
        xx = x if rel else 1 - x
        cc = c if own else 1 - c
        return (t * 4 + xx * 2 + cc) * 2 + half

    def remote(src, dst, send, recv, device):
        return pltpu.make_async_remote_copy(
            src_ref=src, dst_ref=dst, send_sem=send, recv_sem=recv, device_id=device, device_id_type=MESH)

    def core_copy(j):
        return remote(core_out.at[j], core_in.at[j], core_send.at[j], core_recv.at[j], sibling)

    def x_copy(t):
        return remote(x_out.at[t], x_in.at[t], x_send.at[t], x_recv.at[t], beside)

    def lanes(half):
        return pl.ds(half * 256, 256)

    def out_copy(u, half):
        return pltpu.make_async_copy(gathered.at[u], out_ref.at[u // 2, :, lanes(half)], out_sem.at[u])

    def z_copy(k, way):
        return remote(z_out.at[k], z_in.at[way, k], z_send.at[k], z_recv.at[way, k],
                      (me + 4 if way == 0 else me - 4, pix))

    def partial(u, half):
        value = grads_ref[u // 2, :, lanes(half)]
        return (jnp.dot(high_ref[...], value, preferred_element_type=jnp.float32)
                + jnp.dot(low_ref[...], value, preferred_element_type=jnp.float32))

    def nth(i):
        return (i % 2) * (i // 2) + (1 - i % 2) * (3 - i // 2)

    def send_core(half, rel):
        @pl.loop(0, 4)
        def _(i):
            t = nth(i)
            j = (t * 2 + rel) * 2 + half
            core_out[j] = partial(unit(half, t, rel, False), half).astype(jnp.bfloat16)
            core_copy(j).start()

    def keep(half, rel):
        @pl.loop(0, 4)
        def _(i):
            t = nth(i)
            j = (t * 2 + rel) * 2 + half
            value = partial(unit(half, t, rel, True), half)
            core_copy(j).wait_recv()
            value = value + core_in[j].astype(jnp.float32)
            if half == 0 and rel == 0:
                x_out[t] = value.astype(jnp.bfloat16)
                x_copy(t).start()
            else:
                held[item_of(half, t, rel)] = value
            if half == 1:
                k = item_of(half, t, rel)

                @pl.when((z == 0) & (t > 0))
                def _():
                    z_out[k] = value.astype(jnp.bfloat16)
                    z_copy(k, 0).start()

                @pl.when((z == 3) & (t < 3))
                def _():
                    z_out[k] = value.astype(jnp.bfloat16)
                    z_copy(k, 1).start()

    send_core(1, 0)
    send_core(0, 0)
    keep(1, 0)
    keep(0, 0)
    send_core(1, 1)
    keep(1, 1)
    send_core(0, 1)
    keep(0, 1)

    squares[...] = jnp.zeros_like(squares)

    def at_hand(u, half):
        out_copy(u, half).start()

        @pl.loop(0, 8)
        def _(i):
            rows = pl.ds(pl.multiple_of(i * 32, 32), 32)
            lower = pl.ds(pl.multiple_of(i * 32 + 256, 32), 32)
            re = gathered[u, rows, :].astype(jnp.float32)
            im = gathered[u, lower, :].astype(jnp.float32)
            both = re * re + im * im
            squares[rows, :] += both[:, :128] + both[:, 128:]

    def add_up(target, at, sources, weight):
        @pl.loop(0, 16)
        def _(i):
            rows = pl.ds(pl.multiple_of(i * 32, 32), 32)
            value = None
            for ref, index in sources:
                term = ref[index + (rows, slice(None))].astype(jnp.float32)
                value = term if value is None else value + term
            if weight is not None:
                value = value * weight_ref[weight]
            target[at, rows, :] = value.astype(jnp.bfloat16)

    begin = starts()

    def run(zz):
        sent = []
        events = []

        def b_copy():
            return remote(b_out.at[0], b_in.at[0], b_send.at[0], b_recv.at[0], beside)

        def gather_copy(u, way):
            device = (None, None, beside, sibling)[way] or (me + 4 if way == 0 else me - 4, pix)
            return remote(gathered.at[u], gathered.at[u], gather_send.at[way, u], gather_recv.at[u], device)

        def arrive(u):
            gather_copy(u, 3).wait_recv()

        def start(copy):
            copy.start()
            sent.append(copy)

        def onward(u, ways):
            for way in ways:
                start(gather_copy(u, way))

        def z_sources(half, t, rel):
            k = item_of(half, t, rel)
            sources = [(held, (k,))]
            if half == 0:
                x_copy(t).wait_recv()
                sources.append((x_in, (t,)))
            if zz > 0 and t >= zz:
                z_copy(k, 0).wait_recv()
                sources.append((z_in, (0, k)))
            if zz < 3 and t <= zz:
                z_copy(k, 1).wait_recv()
                sources.append((z_in, (1, k)))
            return sources

        def away(t):
            ways = []
            if zz < 3 and t <= zz:
                ways.append(0)
            if zz > 0 and t >= zz:
                ways.append(1)
            return ways

        def pass_on(half, t, rel):
            k = item_of(half, t, rel)
            add_up(z_out, k, z_sources(half, t, rel), None)
            start(z_copy(k, 0 if t > zz else 1))

        def cross():
            add_up(b_out, 0, z_sources(1, zz, 0), None)
            start(b_copy())

        def finish(half):
            sources = z_sources(half, zz, 1)
            if half == 1:
                b_copy().wait_recv()
                sources.append((b_in, (0,)))
            u = unit(half, zz, 1, True)
            add_up(gathered, u, sources, u)
            onward(u, [2] + away(zz) + [3])
            at_hand(u, half)

        def forward(half, t, rel, ways):
            u = unit(half, t, rel, True)
            arrive(u)
            onward(u, ways + [3])
            at_hand(u, half)

        def from_core(half, t, rel):
            u = unit(half, t, rel, False)
            arrive(u)
            at_hand(u, half)

        def put(step, rank, action, *args):
            events.append((step, rank, len(events), action, args))

        def got(step, half, t, rel):
            put(step + 2, 3, from_core, half, t, rel)

        ends = {}
        for half, t, rel in ORDER:
            up, down = begin[half, t, rel]
            ends[half, t, rel] = max(up + t if t > 0 else 0, down + 3 - t if t < 3 else 0)
            if half == 1 and t != zz and zz in (0, 3):
                sent.append(z_copy(item_of(half, t, rel), 0 if zz == 0 else 1))
            elif t != zz:
                put(up + zz if t > zz else down + 3 - zz, 0, pass_on, half, t, rel)
        for t in range(4):
            far = abs(zz - t)
            step = ends[0, t, 1]
            if far == 0:
                put(step, 1, finish, 0)
            else:
                put(step + far, 1, forward, 0, t, 1, [2] + away(t))
            got(step + far, 0, t, 1)
            put(step + far + 1, 2, forward, 0, t, 0, [])
            got(step + far + 1, 0, t, 0)
            step = max(ends[1, t, 1], ends[1, t, 0] + 1)
            if far == 0:
                put(ends[1, t, 0], 0, cross)
                put(step, 1, finish, 1)
            else:
                put(step + far, 1, forward, 1, t, 1, away(t))
            got(step + far, 1, t, 1)
            put(step + far + 1, 1, forward, 1, t, 0, away(t))
            got(step + far + 1, 1, t, 0)
        for event in sorted(events, key=lambda entry: entry[:3]):
            event[3](*event[4])
        for copy in sent:
            copy.wait_send()

    for zz in range(4):
        pl.when(z == zz)(lambda zz=zz: run(zz))

    y_copy = remote(squares, y_in, y_send, y_recv, across)
    y_copy.start()

    @pl.loop(0, 16)
    def _(j):
        core_copy(j).wait_send()

    @pl.loop(0, 4)
    def _(t):
        x_copy(t).wait_send()

    @pl.loop(0, 16)
    def _(r):
        out_copy(2 * r, 0).wait()
        out_copy(2 * r + 1, 1).wait()

    y_copy.wait()
    total_ref[...] = squares[...] + y_in[...]


def gathered_coefficients(units, table, weight):
    high, low = split_parts(table)
    rows, cols = units.shape[1], units.shape[2] // 2
    block = lambda n: pltpu.VMEM((n, rows, cols), jnp.bfloat16)
    dma = pltpu.SemaphoreType.DMA
    vmem = pl.BlockSpec(memory_space=pltpu.VMEM)
    return pl.pallas_call(
        reduce_gather,
        out_shape=(jax.ShapeDtypeStruct(units.shape, jnp.bfloat16),
                   jax.ShapeDtypeStruct((rows // 2, 128), jnp.float32)),
        in_specs=[vmem] * 4,
        out_specs=(pl.BlockSpec(memory_space=pl.ANY), vmem),
        scratch_shapes=[
            block(16), block(16), pltpu.VMEM((12, rows, cols), jnp.float32), block(4), block(4),
            block(12), pltpu.VMEM((2, 12, rows, cols), jnp.bfloat16), block(1), block(1), block(32),
            pltpu.VMEM((rows // 2, 128), jnp.float32), pltpu.VMEM((rows // 2, 128), jnp.float32),
            dma((16,)), dma((16,)), dma((4,)), dma((4,)), dma((12,)), dma((2, 12)), dma((1,)), dma((1,)),
            dma((4, 32)), dma((32,)), dma((32,)), dma, dma,
        ],
        compiler_params=pltpu.CompilerParams(
            collective_id=0, has_side_effects=True, vmem_limit_bytes=58 * 2**20),
    )(units, high, low, weight)


def rows_first(grads_ref, units_ref, spread):
    angles, rows, cols = grads_ref.shape
    for lane in range(cols // 128):
        span = slice(lane * 128, lane * 128 + 128)
        spread[lane] = grads_ref[:, :, span].astype(jnp.float32).reshape(angles * rows, 128)
        for row in range(rows):
            units_ref[row, :, span] = spread[lane, pl.ds(row, angles, stride=rows), :].astype(jnp.bfloat16)


def by_rows(flat):
    angles, rows, cols = flat.shape
    block = 128
    return pl.pallas_call(
        rows_first,
        grid=(angles // block,),
        out_shape=jax.ShapeDtypeStruct((rows, angles, cols), jnp.bfloat16),
        in_specs=[pl.BlockSpec((block, rows, cols), lambda i: (i, 0, 0))],
        out_specs=pl.BlockSpec((rows, block, cols), lambda i: (0, i, 0)),
        scratch_shapes=[pltpu.VMEM((cols // 128, block * rows, 128), jnp.float32)],
        compiler_params=pltpu.CompilerParams(vmem_limit_bytes=40 * 2**20),
    )(flat)


def synthesis(back_ref, every_ref, update_ref, spread):
    angles, rows, cols = update_ref.shape

    @pl.loop(0, rows)
    def _(row):
        value = jnp.dot(back_ref[...], every_ref[row], preferred_element_type=jnp.float32)
        for lane in range(cols // 128):
            spread[lane, pl.ds(row, angles, stride=rows), :] = value[:, lane * 128:lane * 128 + 128]

    for lane in range(cols // 128):
        span = slice(lane * 128, lane * 128 + 128)
        update_ref[:, :, span] = spread[lane].reshape(angles, rows, 128).astype(jnp.bfloat16)


def synthesized(back, every):
    angles, depth = back.shape
    rows, _, cols = every.shape
    block = 256
    return pl.pallas_call(
        synthesis,
        grid=(angles // block,),
        out_shape=jax.ShapeDtypeStruct((angles, rows, cols), jnp.bfloat16),
        in_specs=[pl.BlockSpec((block, depth), lambda i: (i, 0)),
                  pl.BlockSpec((rows, depth, cols), lambda i: (0, 0, 0))],
        out_specs=pl.BlockSpec((block, rows, cols), lambda i: (i, 0, 0)),
        scratch_shapes=[pltpu.VMEM((cols // 128, block * rows, 128), jnp.float32)],
        compiler_params=pltpu.CompilerParams(vmem_limit_bytes=50 * 2**20),
    )(back, every)


def kernel_path(grads, circle_pos, harmonics, support):
    angle_local, row_pix, col_count = grads.shape[1:]
    angle_count = circle_pos.shape[0]
    kept_count = harmonics.shape[0]
    halves, lanes = 2, col_count // 2
    me = lax.axis_index("ang")
    positions = lax.dynamic_slice_in_dim(circle_pos, me * angle_local, angle_local, 0)
    table = phase_table(harmonics, positions, angle_count)
    units = by_rows(grads.reshape(2 * angle_local, row_pix, col_count))
    weight = lax.dynamic_slice_in_dim(support, lax.axis_index("pix") * row_pix, row_pix, 0).astype(jnp.float32)
    weight = (weight * (1.0 / math.sqrt(angle_count))).reshape(row_pix * halves, 1, lanes)
    every, squares = gathered_coefficients(units, table, weight)
    cell_count = float(row_pix * lax.axis_size("pix") * col_count)
    harmonic_rms = jnp.sqrt(jnp.sum(squares, axis=1) / cell_count + 1e-06)
    scale = (1.0 / math.sqrt(kept_count)) / harmonic_rms
    back = table * jnp.concatenate((scale, scale))[:, None]
    update = synthesized(back.T.astype(jnp.bfloat16), every)
    return (update.reshape(grads.shape), harmonic_rms)


def chosen(grads, circle_pos, harmonics, support):
    sizes = (lax.axis_size("ang"), lax.axis_size("pix"), harmonics.shape[0]) + grads.shape[1:]
    fits = sizes == (16, 2, 256, 256, 16, 512)
    return (kernel_path if fits else body)(grads, circle_pos, harmonics, support)


def solution(mesh):
    return jax.shard_map(
        chosen,
        mesh=mesh,
        in_specs=(P(None, "ang", "pix", None), P(), P(), P()),
        out_specs=(P(None, "ang", "pix", None), P()),
        check_vma=False,
    )
```
